128 devices in a mesh: frame: 4 (over z_hi, core), vox: 32 (over x, z_lo, y).
Axes of the slice: x: 4, y: 4, z: 4 (z_hi: 2, z_lo: 2; z = z_hi * 2 + z_lo), core: 2. Of those that a mesh axis runs over, the one named last changes fastest.
Arguments:
- echoes: bfloat16 [32, 1024, 2048], P('frame', 'vox'), may hold values from -12 to 12
- delays: int32 [128, 1024], P(None, 'vox'), may hold values from 0 to 1920
- apod: bfloat16 [128, 1024], P(None, 'vox'), may hold values from 0.0099487305 to 0.099609375
- pattern: int32 [128, 32], replicated, may hold values from 0 to 1, as said below
- start_block: float32 [32, 16], replicated, may hold values from -6 to 6
- clutter_rank: int32 [1], replicated, may hold values from 2 to 16
Outputs:
- filtered: float32 [32, 16384], P(None, ('frame', 'vox'))
The draws below stay inside these ranges and needn't reach their ends.
Inputs may be any that keep to these rules, and one draw needn't show every extreme that they name: Call the blocks b with (b) % 32 == r the blocks of r (4 of them). For every element block c and every r, between 1 and 2 blocks of r have pattern[b, c] = 1; in every draw some r has exactly 2 such blocks for every c.
All inputs are finite; a program needn't handle non-finite values.
Results may differ from the reference program's by a relative error of at most 0.00035.
Values sent between devices are 32-bit elements; how exact they have to be, the bound alone decides.
No kernel may reach another device: no remote copies, remote signals or barrier semaphores. Data moves between devices by JAX's collectives and lax.ppermute only.
A program may use at most 128 MiB of HBM per device.

```python
import math
import jax
import jax.numpy as jnp
from jax import lax

ELEM = 1024
SAMP = 2048
VB = 128
KMAX = 16
ITERS = 1
FRAMES = 32
VOX = 16384
NBLK = 128
NEB = 32
CB = 1
BPD = 4
KB = 2


def draw_pattern(key, part):
    key = jax.random.fold_in(key, 7)
    key_count, key_full, key_order = jax.random.split(key, 3)
    counts = jax.random.randint(key_count, (NEB, NEB), KB // 2, KB + 1)
    chosen = jax.random.randint(key_full, (), 0, NEB)
    counts = jnp.where(jnp.arange(NEB)[None, :] == chosen, KB, counts)
    order_keys = jax.random.split(key_order, NEB * NEB)
    orders = jax.vmap(lambda single: jax.random.permutation(single, BPD))(order_keys)
    ranks = jnp.argsort(orders, axis=1).reshape(NEB, NEB, BPD)
    marked = (ranks < counts[:, :, None]).astype(jnp.int32)
    marked = marked.reshape(NEB, NEB, BPD // CB, CB)
    return jnp.transpose(marked, (2, 1, 3, 0)).reshape(NBLK, NEB)


def draw_echoes(key, part):
    key = jax.random.fold_in(key, 11)
    key_noise, key_shape, key_phase, key_rate = jax.random.split(key, 4)
    noise = jax.random.normal(key_noise, (FRAMES, ELEM, SAMP), jnp.float32)
    moments = jnp.arange(FRAMES, dtype=jnp.float32) / FRAMES
    phases = jax.random.uniform(key_phase, (3,), jnp.float32, 0.0, 6.2831853)
    rates = jax.random.uniform(key_rate, (3,), jnp.float32, 0.5, 2.0)
    profiles = 2.0 * jnp.cos(6.2831853 * rates[:, None] * moments[None, :] + phases[:, None])
    tissue = jax.random.normal(key_shape, (3, ELEM, SAMP), jnp.float32)
    total = noise
    for component in range(3):
        total = total + profiles[component][:, None, None] * tissue[component][None]
    return jnp.clip(total, -12.0, 12.0).astype(jnp.bfloat16)


def touch_ends(entries, own_key, low, largest):
    longest = entries.shape.index(max(entries.shape))
    spots = []
    for shift in (0, 1):
        where = [jax.random.randint(jax.random.fold_in(own_key, axis), (), 0, length) for axis, length in enumerate(entries.shape)]
        where[longest] = (where[longest] + shift) % entries.shape[longest]
        spots.append(tuple(where))
    return entries.at[spots[0]].set(low).at[spots[1]].set(largest)


def block_scale(stream_key, shape, cuts, smallest, top_value):
    factor_of, own = 1.0, jax.random.fold_in(stream_key, 6)
    for dim, shards_of in cuts:
        heights = jnp.exp(jax.random.uniform(jax.random.fold_in(own, dim), (shards_of,), jnp.float32, smallest / len(cuts), top_value / len(cuts)))
        factor_of = factor_of * jnp.repeat(heights, shape[dim] // shards_of).reshape([-1 if axis == dim else 1 for axis in range(len(shape))])
    return factor_of


def gaussian(key, extent, deviation, reach, kind=jnp.bfloat16):
    return jnp.clip(deviation * jax.random.normal(key, extent, jnp.float32), -reach, reach).astype(kind)


def setup_inputs(seed: int = 0) -> dict:
    seeds = jax.random.split(jax.random.key(seed), 7)
    return {
        "echoes": draw_echoes(jax.random.fold_in(seeds[6], 71), 0),
        "delays": touch_ends(jax.random.randint(seeds[1], (NBLK, ELEM), 0, SAMP - VB + 1), jax.random.fold_in(seeds[1], 1), 0, SAMP - VB).astype(jnp.int32),
        "apod": jnp.clip(jnp.exp(math.log(0.099609375) - 2.3038113 * jax.random.uniform(seeds[2], (NBLK, ELEM), jnp.float32) ** block_scale(seeds[2], (NBLK, ELEM), ((1, 32),), -0.2, 0.2)), 0.0099487305, 0.099609375).astype(jnp.bfloat16),
        "pattern": draw_pattern(jax.random.fold_in(seeds[6], 71), 0),
        "start_block": gaussian(seeds[4], (FRAMES, KMAX), 1.0, 6.0, jnp.float32),
        "clutter_rank": jax.random.randint(seeds[5], (1,), 2, KMAX + 1).astype(jnp.int32),
    }


def orthonormal(block):
    columns = []
    for column in range(block.shape[1]):
        vector = block[:, column]
        for earlier in columns:
            vector = vector - jnp.sum(earlier * vector) * earlier
        vector = vector * lax.rsqrt(jnp.sum(vector * vector) + 1e-06)
        columns.append(vector)
    return jnp.stack(columns, axis=1)

def reference(echoes, delays, apod, pattern, start_block, clutter_rank):
    group_width = ELEM // NEB
    weights = apod.astype(jnp.float32) * jnp.repeat(pattern, group_width, axis=1).astype(jnp.float32)
    offsets = jnp.arange(VB, dtype=jnp.int32)

    def one_block(inputs):
        delay_row, weight_row = inputs
        sample_index = delay_row[:, None] + offsets[None, :]
        sample_index = jnp.broadcast_to(sample_index[None], (FRAMES, ELEM, VB))
        samples = jnp.take_along_axis(echoes, sample_index, axis=2).astype(jnp.float32)
        return jnp.einsum('fev,e->fv', samples, weight_row)
    tiles = lax.map(one_block, (delays, weights))
    image = jnp.transpose(tiles, (1, 0, 2)).reshape(FRAMES, VOX)
    gram_matrix = jnp.dot(image, image.T, precision=lax.Precision.HIGHEST)
    basis = orthonormal(jnp.dot(gram_matrix, start_block, precision=lax.Precision.HIGHEST))
    for sweep in range(ITERS):
        basis = orthonormal(jnp.dot(gram_matrix, basis, precision=lax.Precision.HIGHEST))
    kept_mask = (jnp.arange(KMAX, dtype=jnp.int32) < clutter_rank[0]).astype(jnp.float32)
    coeffs = jnp.dot(basis.T, image, precision=lax.Precision.HIGHEST) * kept_mask[:, None]
    return image - jnp.dot(basis, coeffs, precision=lax.Precision.HIGHEST)
```

```python
import jax
import jax.numpy as jnp
from jax import lax
from jax.experimental import pallas as pl
from jax.experimental.pallas import tpu as pltpu
from jax.sharding import PartitionSpec as P

VB = 128
SLOTS = 2
STEP = 4
HIGHEST = lax.Precision.HIGHEST


def dot(a, b, da, db):
    return lax.dot_general(
        a, b, (((da,), (db,)), ((), ())), precision=HIGHEST, preferred_element_type=jnp.float32
    )


def turned(value, index):
    return jnp.take_along_axis(value, index, axis=1, mode="promise_in_bounds")


def beam_kernel(
    pattern_in, delays_in, apod_in, echoes_in, out,
    raw, tiles, delays, table, marks, rows, row_words, turns, turn_words, rest_wide, weight_wide,
    blocks, places, sems, echo_sems,
):
    f_dev, group, samples = echoes_in.shape
    n_tiles = samples // VB
    tile_rows = group * f_dev
    n_blocks = marks.shape[1]
    n_vox = out.shape[0] // SLOTS
    n_own = n_blocks // n_vox
    column = lax.axis_index("vox")
    copy_delays = pltpu.make_async_copy(delays_in, delays, sems.at[0])
    copy_marks = pltpu.make_async_copy(pattern_in, marks, sems.at[1])
    copy_apod = pltpu.make_async_copy(apod_in, table.at[group : 2 * group], sems.at[2])
    copy_delays.start()
    copy_marks.start()
    copy_apod.start()
    copies = []
    for f in range(f_dev):
        own_rows = pl.ds(f * group, group)
        copies.append(pltpu.make_async_copy(echoes_in.at[f], raw.at[own_rows], echo_sems.at[f]))
        copies[f].start()

    copy_delays.wait()
    element = lax.broadcasted_iota(jnp.int32, delays.shape, 0)
    rows[...] = lax.shift_right_logical(delays[...], 7) * group + element
    put_rows = pltpu.make_async_copy(rows, row_words, sems.at[3])
    put_rows.start()
    turns[...] = (VB - delays[...]) & (VB - 1)
    put_turns = pltpu.make_async_copy(turns, turn_words, sems.at[4])
    put_turns.start()
    table[0:group, :] = (delays[...] & (VB - 1)).astype(table.dtype)

    copy_marks.wait()

    count = jnp.int32(0)
    for r in range(n_vox):
        first = jnp.int32(n_own)
        second = jnp.int32(n_own)
        for i in range(n_own - 1, -1, -1):
            marked = marks[column, i * n_vox + r] == 1
            second = jnp.where(marked, first, second)
            first = jnp.where(marked, i, first)
        blocks[count] = first * n_vox + r
        places[count] = r * SLOTS
        blocks[count + 1] = second * n_vox + r
        places[count + 1] = r * SLOTS + 1
        out[r * SLOTS + 1] = jnp.zeros(out.shape[1:], jnp.float32)
        count = count + jnp.where(second < n_own, 2, 1)
    for i in range(2 * STEP - 1):
        blocks[count + i] = blocks[count - 1]
        places[count + i] = places[count - 1]

    copy_apod.wait()
    lane = lax.broadcasted_iota(jnp.int32, (8, VB), 1)

    block_row = lax.broadcasted_iota(jnp.int32, (n_blocks, VB), 0)

    def spread(s, half):
        for i in range(STEP):
            pick = jnp.where(block_row == blocks[s * STEP + i], 1.0, 0.0).astype(table.dtype)
            wide = jnp.dot(table[...], pick, preferred_element_type=jnp.float32)
            at = pl.ds((half * STEP + i) * group, group)
            rest_wide[at, :] = wide[0:group].astype(jnp.int32)
            weight_wide[at, :] = wide[group : 2 * group]

    spread(0, 0)

    tiles[n_tiles * group : (n_tiles + 1) * group] = jnp.zeros((group, f_dev, VB), jnp.float32)
    to_row = lax.broadcasted_iota(jnp.int32, (tile_rows, tile_rows), 0)
    from_row = lax.broadcasted_iota(jnp.int32, (tile_rows, tile_rows), 1)
    moves = (to_row & (f_dev - 1)) * group + lax.shift_right_logical(to_row, 3) == from_row
    moves = jnp.where(moves, 1.0, 0.0).astype(raw.dtype)
    for f in range(f_dev):
        copies[f].wait()
    for q in range(0, n_tiles, 2):
        pair = jnp.dot(
            moves, raw[:, q * VB : (q + 2) * VB], preferred_element_type=jnp.float32
        )
        for half in range(2):
            tiles[(q + half) * group : (q + half + 1) * group] = pair[
                :, half * VB : (half + 1) * VB
            ].reshape(group, f_dev, VB)

    put_rows.wait()
    put_turns.wait()

    def step(s, carry):
        half = s & 1
        own = [blocks[s * STEP + i] for i in range(STEP)]
        totals = [None] * STEP
        for e in range(group):
            for i in range(STEP):
                row = row_words[e, own[i]]
                at = (half * STEP + i) * group + e
                low = tiles[row]
                high = tiles[row + group]
                rest = rest_wide[pl.ds(at, 1), :]
                weight = weight_wide[pl.ds(at, 1), :]
                mixed = jnp.where(lane >= rest, low, high)
                term = pltpu.roll(mixed, turn_words[e, own[i]], 1) * weight
                totals[i] = term if e == 0 else totals[i] + term
        for i in range(STEP):
            out[places[s * STEP + i]] = totals[i]
        spread(s + 1, 1 - half)
        return carry

    lax.fori_loop(0, (count + STEP - 1) // STEP, step, 0)


def place_kernel(rank, marks, parts, out, kept, picks):
    n_vox = parts.shape[0]
    n_own = out.shape[0]
    r = lax.axis_index("vox")
    kept[...] = jnp.where(
        lax.broadcasted_iota(jnp.int32, kept.shape, 0) < rank[0], jnp.float32(1), jnp.float32(0)
    )
    for c in range(0, n_vox, 8):
        before = jnp.zeros((8, VB), jnp.int32)
        for i in range(n_own):
            mark = turned(marks[c : c + 8, :], jnp.full((8, VB), i * n_vox + r, jnp.int32))
            for s in range(SLOTS):
                hit = (mark == 1) & (before == s)
                picks[i, s, c : c + 8, :] = jnp.where(hit, jnp.float32(1), jnp.float32(0))
            before = before + mark
    for i in range(n_own):
        totals = []
        for s in range(SLOTS):
            for half in range(2):
                total = None
                for c in range(half, n_vox, 2):
                    term = parts[c, s] * picks[i, s, c : c + 1, :]
                    total = term if total is None else total + term
                totals.append(total)
        out[i] = (totals[0] + totals[1]) + (totals[2] + totals[3])


def gram_kernel(*refs):
    received, (image, grams, parts) = refs[:-3], refs[-3:]
    n_frame, n_own, f_dev, _ = parts.shape
    own = lax.axis_index("frame")
    for flip in range(n_frame):
        parts[own ^ flip] = received[flip][...]
    spans = [
        jnp.concatenate([parts[f, i] for f in range(n_frame)], axis=0) for i in range(n_own)
    ]
    wide = jnp.concatenate(spans, axis=1)
    gram = dot(wide, wide, 1, 1)
    packed = jnp.concatenate([gram[f * f_dev : (f + 1) * f_dev] for f in range(n_frame)], axis=1)
    for i in range(grams.shape[0]):
        grams[i] = packed
    for f in range(n_frame):
        image[f * f_dev : (f + 1) * f_dev] = parts[f, own]


def orthonormal_rows(z):
    row = lax.broadcasted_iota(jnp.int32, (z.shape[0], 1), 0)
    for k in range(z.shape[0]):
        current = jnp.broadcast_to(z[k : k + 1], z.shape)
        inner = jnp.sum(z * current, axis=1, keepdims=True)
        scale = lax.rsqrt(jnp.sum(current * current, axis=1, keepdims=True) + 1e-06)
        share = jnp.where(row > k, inner, 0.0) * (scale * scale)
        z = jnp.where(row == k, current * scale, z - share * current)
    return z


def subspace_kernel(grams, image, start, kept, out, square):
    frames = image.shape[0]
    f_dev = grams.shape[1]
    packed = jnp.sum(grams[...], axis=0)
    square[...] = jnp.zeros_like(square)
    for f in range(frames // f_dev):
        square[f * f_dev : (f + 1) * f_dev, 0:frames] = packed[:, f * frames : (f + 1) * frames]
    gram = square[...]
    basis = orthonormal_rows(dot(start[...], gram[0:frames], 1, 0))
    basis = orthonormal_rows(dot(basis, gram, 1, 0))[:, 0:frames]
    own = image[...]
    coeffs = dot(basis, own, 1, 0) * kept[...]
    out[...] = own - dot(basis, coeffs, 0, 0)


def per_device(echoes, delays, apod, pattern, start_block, clutter_rank):
    n_vox = lax.axis_size("vox")
    n_frame = lax.axis_size("frame")
    f_dev, group, samples = echoes.shape
    frames = f_dev * n_frame
    n_blocks = delays.shape[0]
    n_own = n_blocks // n_vox
    n_tiles = samples // VB
    f32, i32 = jnp.float32, jnp.int32
    vmem = pl.BlockSpec(memory_space=pltpu.VMEM)
    smem = pl.BlockSpec(memory_space=pltpu.SMEM)
    hbm = pl.BlockSpec(memory_space=pltpu.HBM)
    params = pltpu.CompilerParams(vmem_limit_bytes=32 * 1024 * 1024)
    all_vmem = pltpu.CompilerParams(vmem_limit_bytes=56 * 1024 * 1024)
    slots = pl.pallas_call(
        beam_kernel,
        out_shape=jax.ShapeDtypeStruct((n_vox * SLOTS, f_dev, VB), f32),
        in_specs=[hbm, hbm, hbm, hbm],
        out_specs=vmem,
        scratch_shapes=[
            pltpu.VMEM((f_dev * group, samples), echoes.dtype),
            pltpu.VMEM(((n_tiles + 1) * group, f_dev, VB), f32),
            pltpu.VMEM((group, n_blocks), i32),
            pltpu.VMEM((2 * group, n_blocks), apod.dtype),
            pltpu.SMEM((pattern.shape[1], n_blocks), i32),
            pltpu.VMEM((group, n_blocks), i32),
            pltpu.SMEM((group, n_blocks), i32),
            pltpu.VMEM((group, n_blocks), i32),
            pltpu.SMEM((group, n_blocks), i32),
            pltpu.VMEM((2 * STEP * group, VB), i32),
            pltpu.VMEM((2 * STEP * group, VB), f32),
            pltpu.SMEM((n_vox * SLOTS + 3 * STEP,), i32),
            pltpu.SMEM((n_vox * SLOTS + 3 * STEP,), i32),
            pltpu.SemaphoreType.DMA((5,)),
            pltpu.SemaphoreType.DMA((f_dev,)),
        ],
        compiler_params=all_vmem,
    )(pattern.T, delays.T, apod.T, echoes)
    slots, later_rank = lax.optimization_barrier((slots, clutter_rank))
    parts = lax.all_to_all(slots, "vox", split_axis=0, concat_axis=0, tiled=True)
    placed, kept = pl.pallas_call(
        place_kernel,
        out_shape=(
            jax.ShapeDtypeStruct((n_own, f_dev, VB), f32),
            jax.ShapeDtypeStruct((start_block.shape[1], VB), f32),
        ),
        in_specs=[smem, vmem, vmem],
        out_specs=(vmem, vmem),
        scratch_shapes=[pltpu.VMEM((n_own, SLOTS, n_vox, VB), f32)],
        compiler_params=params,
    )(later_rank, pattern.T, parts.reshape(n_vox, SLOTS, f_dev, VB))

    def flipped(value, flip):
        return lax.ppermute(value, "frame", [(f, f ^ flip) for f in range(n_frame)])

    across = flipped(placed, 2)
    received = [placed, flipped(placed, 1), across, flipped(across, 1)]
    own_image, grams = pl.pallas_call(
        gram_kernel,
        out_shape=(
            jax.ShapeDtypeStruct((frames, VB), f32),
            jax.ShapeDtypeStruct((n_vox, f_dev, VB), f32),
        ),
        in_specs=[vmem] * n_frame,
        out_specs=(vmem, vmem),
        scratch_shapes=[pltpu.VMEM((n_frame, n_own, f_dev, VB), f32)],
        compiler_params=params,
    )(*received)
    grams = lax.all_to_all(grams, "vox", split_axis=0, concat_axis=0, tiled=True)
    return pl.pallas_call(
        subspace_kernel,
        out_shape=jax.ShapeDtypeStruct((frames, VB), f32),
        in_specs=[vmem, vmem, vmem, vmem],
        out_specs=vmem,
        scratch_shapes=[pltpu.VMEM((VB, VB), f32)],
        compiler_params=params,
    )(grams, own_image, start_block.T, kept)


def solution(mesh):
    placed = (P("frame", "vox", None), P(None, "vox"), P(None, "vox"), P(), P(), P())
    return jax.shard_map(
        per_device, mesh=mesh, in_specs=placed, out_specs=P(None, ("frame", "vox")), check_vma=False
    )
```

```python
import jax
import jax.numpy as jnp
from jax import lax
from jax.experimental import pallas as pl
from jax.experimental.pallas import tpu as pltpu
from jax.sharding import PartitionSpec as P

VB = 128
SLOTS = 2
STEP = 4
HIGHEST = lax.Precision.HIGHEST


def dot(a, b, da, db):
    return lax.dot_general(
        a, b, (((da,), (db,)), ((), ())), precision=HIGHEST, preferred_element_type=jnp.float32
    )


def turned(value, index):
    return jnp.take_along_axis(value, index, axis=1, mode="promise_in_bounds")


def beam_kernel(
    pattern_in, delays_in, apod_in, echoes_in, out,
    raw, tiles, delays, table, marks, rows, row_words, turns, turn_words, rest_wide, weight_wide,
    blocks, places, sems, echo_sems,
):
    f_dev, group, samples = echoes_in.shape
    n_tiles = samples // VB
    tile_rows = group * f_dev
    n_blocks = marks.shape[1]
    n_vox = out.shape[0] // SLOTS
    n_own = n_blocks // n_vox
    column = lax.axis_index("vox")
    copy_delays = pltpu.make_async_copy(delays_in, delays, sems.at[0])
    copy_marks = pltpu.make_async_copy(pattern_in, marks, sems.at[1])
    copy_apod = pltpu.make_async_copy(apod_in, table.at[group : 2 * group], sems.at[2])
    copy_delays.start()
    copy_marks.start()
    copy_apod.start()
    copies = []
    for f in range(f_dev):
        own_rows = pl.ds(f * group, group)
        copies.append(pltpu.make_async_copy(echoes_in.at[f], raw.at[own_rows], echo_sems.at[f]))
        copies[f].start()

    copy_delays.wait()
    element = lax.broadcasted_iota(jnp.int32, delays.shape, 0)
    rows[...] = lax.shift_right_logical(delays[...], 7) * group + element
    put_rows = pltpu.make_async_copy(rows, row_words, sems.at[3])
    put_rows.start()
    turns[...] = (VB - delays[...]) & (VB - 1)
    put_turns = pltpu.make_async_copy(turns, turn_words, sems.at[4])
    put_turns.start()
    table[0:group, :] = (delays[...] & (VB - 1)).astype(table.dtype)

    copy_marks.wait()

    count = jnp.int32(0)
    for r in range(n_vox):
        first = jnp.int32(n_own)
        second = jnp.int32(n_own)
        for i in range(n_own - 1, -1, -1):
            marked = marks[column, i * n_vox + r] == 1
            second = jnp.where(marked, first, second)
            first = jnp.where(marked, i, first)
        blocks[count] = first * n_vox + r
        places[count] = r * SLOTS
        blocks[count + 1] = second * n_vox + r
        places[count + 1] = r * SLOTS + 1
        out[r * SLOTS + 1] = jnp.zeros(out.shape[1:], jnp.float32)
        count = count + jnp.where(second < n_own, 2, 1)
    for i in range(2 * STEP - 1):
        blocks[count + i] = blocks[count - 1]
        places[count + i] = places[count - 1]

    copy_apod.wait()
    lane = lax.broadcasted_iota(jnp.int32, (8, VB), 1)

    block_row = lax.broadcasted_iota(jnp.int32, (n_blocks, VB), 0)

    def spread(s, half):
        for i in range(STEP):
            pick = jnp.where(block_row == blocks[s * STEP + i], 1.0, 0.0).astype(table.dtype)
            wide = jnp.dot(table[...], pick, preferred_element_type=jnp.float32)
            at = pl.ds((half * STEP + i) * group, group)
            rest_wide[at, :] = wide[0:group].astype(jnp.int32)
            weight_wide[at, :] = wide[group : 2 * group]

    spread(0, 0)

    tiles[n_tiles * group : (n_tiles + 1) * group] = jnp.zeros((group, f_dev, VB), jnp.float32)
    to_row = lax.broadcasted_iota(jnp.int32, (tile_rows, tile_rows), 0)
    from_row = lax.broadcasted_iota(jnp.int32, (tile_rows, tile_rows), 1)
    moves = (to_row & (f_dev - 1)) * group + lax.shift_right_logical(to_row, 3) == from_row
    moves = jnp.where(moves, 1.0, 0.0).astype(raw.dtype)
    for f in range(f_dev):
        copies[f].wait()
    for q in range(0, n_tiles, 2):
        pair = jnp.dot(
            moves, raw[:, q * VB : (q + 2) * VB], preferred_element_type=jnp.float32
        )
        for half in range(2):
            tiles[(q + half) * group : (q + half + 1) * group] = pair[
                :, half * VB : (half + 1) * VB
            ].reshape(group, f_dev, VB)

    put_rows.wait()
    put_turns.wait()

    def step(s, carry):
        half = s & 1
        own = [blocks[s * STEP + i] for i in range(STEP)]
        totals = [None] * STEP
        for e in range(group):
            for i in range(STEP):
                row = row_words[e, own[i]]
                at = (half * STEP + i) * group + e
                low = tiles[row]
                high = tiles[row + group]
                rest = rest_wide[pl.ds(at, 1), :]
                weight = weight_wide[pl.ds(at, 1), :]
                mixed = jnp.where(lane >= rest, low, high)
                if e % 3 == 0:
                    mixed = turned(mixed, (lane + rest) & (VB - 1))
                else:
                    mixed = pltpu.roll(mixed, turn_words[e, own[i]], 1)
                term = mixed * weight
                totals[i] = term if e == 0 else totals[i] + term
        for i in range(STEP):
            out[places[s * STEP + i]] = totals[i]
        spread(s + 1, 1 - half)
        return carry

    lax.fori_loop(0, (count + STEP - 1) // STEP, step, 0)


def place_kernel(rank, marks, parts, out, kept, picks):
    n_vox = parts.shape[0]
    n_own = out.shape[0]
    r = lax.axis_index("vox")
    kept[...] = jnp.where(
        lax.broadcasted_iota(jnp.int32, kept.shape, 0) < rank[0], jnp.float32(1), jnp.float32(0)
    )
    for c in range(0, n_vox, 8):
        before = jnp.zeros((8, VB), jnp.int32)
        for i in range(n_own):
            mark = turned(marks[c : c + 8, :], jnp.full((8, VB), i * n_vox + r, jnp.int32))
            for s in range(SLOTS):
                hit = (mark == 1) & (before == s)
                picks[i, s, c : c + 8, :] = jnp.where(hit, jnp.float32(1), jnp.float32(0))
            before = before + mark
    for i in range(n_own):
        totals = []
        for s in range(SLOTS):
            for half in range(2):
                total = None
                for c in range(half, n_vox, 2):
                    term = parts[c, s] * picks[i, s, c : c + 1, :]
                    total = term if total is None else total + term
                totals.append(total)
        out[i] = (totals[0] + totals[1]) + (totals[2] + totals[3])


def gram_kernel(*refs):
    received, (image, grams, parts) = refs[:-3], refs[-3:]
    n_frame, n_own, f_dev, _ = parts.shape
    own = lax.axis_index("frame")
    for flip in range(n_frame):
        parts[own ^ flip] = received[flip][...]
    spans = [
        jnp.concatenate([parts[f, i] for f in range(n_frame)], axis=0) for i in range(n_own)
    ]
    wide = jnp.concatenate(spans, axis=1)
    gram = dot(wide, wide, 1, 1)
    packed = jnp.concatenate([gram[f * f_dev : (f + 1) * f_dev] for f in range(n_frame)], axis=1)
    for i in range(grams.shape[0]):
        grams[i] = packed
    for f in range(n_frame):
        image[f * f_dev : (f + 1) * f_dev] = parts[f, own]


def orthonormal(columns):
    count = columns.shape[0]
    for k in range(count):
        current = columns[k]
        scale = lax.rsqrt(jnp.sum(current * current, axis=0, keepdims=True) + 1e-06)
        for j in range(k + 1, count):
            inner = jnp.sum(current * columns[j], axis=0, keepdims=True)
            columns[j] = columns[j] - (inner * (scale * scale)) * current
        columns[k] = current * scale


def subspace_kernel(grams, image, start, kept, out, square, columns):
    frames = image.shape[0]
    f_dev = grams.shape[1]
    count = columns.shape[0]
    packed = jnp.sum(grams[...], axis=0)
    for f in range(frames // f_dev):
        square[f * f_dev : (f + 1) * f_dev, :] = packed[:, f * frames : (f + 1) * frames]
    gram = square[...]
    for source in (start, columns):
        wide = dot(gram, jnp.concatenate([source[k] for k in range(count)], axis=1), 1, 0)
        for k in range(count):
            columns[k] = wide[:, k * VB : (k + 1) * VB]
        orthonormal(columns)
    own = image[...]
    left = own
    for k in range(count):
        coeffs = jnp.sum(columns[k] * own, axis=0, keepdims=True) * kept[k : k + 1, :]
        left = left - columns[k] * coeffs
    out[...] = left


def per_device(echoes, delays, apod, pattern, start_block, clutter_rank):
    n_vox = lax.axis_size("vox")
    n_frame = lax.axis_size("frame")
    f_dev, group, samples = echoes.shape
    frames = f_dev * n_frame
    n_blocks = delays.shape[0]
    n_own = n_blocks // n_vox
    n_tiles = samples // VB
    f32, i32 = jnp.float32, jnp.int32
    vmem = pl.BlockSpec(memory_space=pltpu.VMEM)
    smem = pl.BlockSpec(memory_space=pltpu.SMEM)
    hbm = pl.BlockSpec(memory_space=pltpu.HBM)
    params = pltpu.CompilerParams(vmem_limit_bytes=32 * 1024 * 1024)
    all_vmem = pltpu.CompilerParams(vmem_limit_bytes=56 * 1024 * 1024)
    slots = pl.pallas_call(
        beam_kernel,
        out_shape=jax.ShapeDtypeStruct((n_vox * SLOTS, f_dev, VB), f32),
        in_specs=[hbm, hbm, hbm, hbm],
        out_specs=vmem,
        scratch_shapes=[
            pltpu.VMEM((f_dev * group, samples), echoes.dtype),
            pltpu.VMEM(((n_tiles + 1) * group, f_dev, VB), f32),
            pltpu.VMEM((group, n_blocks), i32),
            pltpu.VMEM((2 * group, n_blocks), apod.dtype),
            pltpu.SMEM((pattern.shape[1], n_blocks), i32),
            pltpu.VMEM((group, n_blocks), i32),
            pltpu.SMEM((group, n_blocks), i32),
            pltpu.VMEM((group, n_blocks), i32),
            pltpu.SMEM((group, n_blocks), i32),
            pltpu.VMEM((2 * STEP * group, VB), i32),
            pltpu.VMEM((2 * STEP * group, VB), f32),
            pltpu.SMEM((n_vox * SLOTS + 3 * STEP,), i32),
            pltpu.SMEM((n_vox * SLOTS + 3 * STEP,), i32),
            pltpu.SemaphoreType.DMA((5,)),
            pltpu.SemaphoreType.DMA((f_dev,)),
        ],
        compiler_params=all_vmem,
    )(pattern.T, delays.T, apod.T, echoes)
    slots, later_rank, later_start = lax.optimization_barrier((slots, clutter_rank, start_block))
    wide_start = jnp.broadcast_to(later_start.T[:, :, None], (start_block.shape[1], frames, VB))
    parts = lax.all_to_all(slots, "vox", split_axis=0, concat_axis=0, tiled=True)
    placed, kept = pl.pallas_call(
        place_kernel,
        out_shape=(
            jax.ShapeDtypeStruct((n_own, f_dev, VB), f32),
            jax.ShapeDtypeStruct((start_block.shape[1], VB), f32),
        ),
        in_specs=[smem, vmem, vmem],
        out_specs=(vmem, vmem),
        scratch_shapes=[pltpu.VMEM((n_own, SLOTS, n_vox, VB), f32)],
        compiler_params=params,
    )(later_rank, pattern.T, parts.reshape(n_vox, SLOTS, f_dev, VB))

    def flipped(value, flip):
        return lax.ppermute(value, "frame", [(f, f ^ flip) for f in range(n_frame)])

    across = flipped(placed, 2)
    received = [placed, flipped(placed, 1), across, flipped(across, 1)]
    own_image, grams = pl.pallas_call(
        gram_kernel,
        out_shape=(
            jax.ShapeDtypeStruct((frames, VB), f32),
            jax.ShapeDtypeStruct((n_vox, f_dev, VB), f32),
        ),
        in_specs=[vmem] * n_frame,
        out_specs=(vmem, vmem),
        scratch_shapes=[pltpu.VMEM((n_frame, n_own, f_dev, VB), f32)],
        compiler_params=params,
    )(*received)
    grams = lax.all_to_all(grams, "vox", split_axis=0, concat_axis=0, tiled=True)
    return pl.pallas_call(
        subspace_kernel,
        out_shape=jax.ShapeDtypeStruct((frames, VB), f32),
        in_specs=[vmem, vmem, vmem, vmem],
        out_specs=vmem,
        scratch_shapes=[
            pltpu.VMEM((frames, frames), f32),
            pltpu.VMEM((start_block.shape[1], frames, VB), f32),
        ],
        compiler_params=params,
    )(grams, own_image, wide_start, kept)


def solution(mesh):
    placed = (P("frame", "vox", None), P(None, "vox"), P(None, "vox"), P(), P(), P())
    return jax.shard_map(
        per_device, mesh=mesh, in_specs=placed, out_specs=P(None, ("frame", "vox")), check_vma=False
    )
```

```python
import jax
import jax.numpy as jnp
from jax import lax
from jax.experimental import pallas as pl
from jax.experimental.pallas import tpu as pltpu
from jax.sharding import PartitionSpec as P

VB = 128
SLOTS = 2
STEP = 4
HIGHEST = lax.Precision.HIGHEST


def dot(a, b, da, db):
    return lax.dot_general(
        a, b, (((da,), (db,)), ((), ())), precision=HIGHEST, preferred_element_type=jnp.float32
    )


def turned(value, index):
    return jnp.take_along_axis(value, index, axis=1, mode="promise_in_bounds")


def beam_kernel(
    pattern_in, delays_in, apod_in, echoes_in, out,
    raw, tiles, delays, apod, marks, rows, row_words, turns, turn_words, weight_wide,
    blocks, places, sems, echo_sems,
):
    f_dev, group, samples = echoes_in.shape
    n_tiles = samples // VB
    tile_rows = group * f_dev
    n_blocks = marks.shape[1]
    n_vox = out.shape[0] // SLOTS
    n_own = n_blocks // n_vox
    column = lax.axis_index("vox")
    copy_delays = pltpu.make_async_copy(delays_in, delays, sems.at[0])
    copy_marks = pltpu.make_async_copy(pattern_in, marks, sems.at[1])
    copy_apod = pltpu.make_async_copy(apod_in, apod, sems.at[2])
    copy_delays.start()
    copy_marks.start()
    copies = []
    for f in range(f_dev):
        own_rows = pl.ds(f * group, group)
        copies.append(pltpu.make_async_copy(echoes_in.at[f], raw.at[own_rows], echo_sems.at[f]))
        copies[f].start()
    copy_apod.start()

    to_row = lax.broadcasted_iota(jnp.int32, (tile_rows, tile_rows), 0)
    from_row = lax.broadcasted_iota(jnp.int32, (tile_rows, tile_rows), 1)
    moves = (to_row & (f_dev - 1)) * group + lax.shift_right_logical(to_row, 3) == from_row
    moves = jnp.where(moves, 1.0, 0.0).astype(raw.dtype)
    tiles[0:group] = jnp.zeros((group, f_dev, VB), jnp.float32)

    copy_delays.wait()
    element = lax.broadcasted_iota(jnp.int32, delays.shape, 0)
    rows[...] = lax.shift_right_logical(delays[...] + (VB - 1), 7) * group + element
    turns[...] = (VB - (delays[...] & (VB - 1))) & (VB - 1)
    put_rows = pltpu.make_async_copy(rows, row_words, sems.at[3])
    put_turns = pltpu.make_async_copy(turns, turn_words, sems.at[4])
    put_rows.start()
    put_turns.start()

    copy_marks.wait()
    for f in range(f_dev):
        copies[f].wait()
    copy_apod.wait()

    for q in range(0, n_tiles, 2):
        pair = jnp.dot(
            moves, raw[:, q * VB : (q + 2) * VB], preferred_element_type=jnp.float32
        )
        for half in range(2):
            tiles[(q + half + 1) * group : (q + half + 2) * group] = pair[
                :, half * VB : (half + 1) * VB
            ].reshape(group, f_dev, VB)

    count = jnp.int32(0)
    for r in range(n_vox):
        first = jnp.int32(n_own)
        second = jnp.int32(n_own)
        for i in range(n_own - 1, -1, -1):
            marked = marks[column, i * n_vox + r] == 1
            second = jnp.where(marked, first, second)
            first = jnp.where(marked, i, first)
        blocks[count] = first * n_vox + r
        places[count] = r * SLOTS
        blocks[count + 1] = second * n_vox + r
        places[count + 1] = r * SLOTS + 1
        out[r * SLOTS + 1] = jnp.zeros(out.shape[1:], jnp.float32)
        count = count + jnp.where(second < n_own, 2, 1)
    for i in range(2 * STEP - 1):
        blocks[count + i] = blocks[count - 1]
        places[count + i] = places[count - 1]

    past = VB - lax.broadcasted_iota(jnp.int32, (f_dev, VB), 1)
    block_row = lax.broadcasted_iota(jnp.int32, (n_blocks, VB), 0)

    def spread(s, half):
        for i in range(STEP):
            pick = jnp.where(block_row == blocks[s * STEP + i], 1.0, 0.0).astype(apod.dtype)
            at = pl.ds((half * STEP + i) * group, group)
            weight_wide[at, :] = jnp.dot(apod[...], pick, preferred_element_type=jnp.float32)

    spread(0, 0)
    put_rows.wait()
    put_turns.wait()

    def step(s, carry):
        half = s & 1
        own = [blocks[s * STEP + i] for i in range(STEP)]
        totals = [None] * STEP
        for e in range(group):
            for i in range(STEP):
                row = row_words[e, own[i]]
                turn = turn_words[e, own[i]]
                mixed = jnp.where(past <= turn, tiles[row], tiles[row + group])
                weight = weight_wide[pl.ds((half * STEP + i) * group + e, 1), :]
                term = pltpu.roll(mixed, turn, 1) * weight
                totals[i] = term if e == 0 else totals[i] + term
        for i in range(STEP):
            out[places[s * STEP + i]] = totals[i]
        spread(s + 1, 1 - half)
        return carry

    lax.fori_loop(0, (count + STEP - 1) // STEP, step, 0)


def place_kernel(rank, marks, parts, out, kept, picks):
    n_vox = parts.shape[0]
    n_own = out.shape[0]
    r = lax.axis_index("vox")
    kept[...] = jnp.where(
        lax.broadcasted_iota(jnp.int32, kept.shape, 0) < rank[0], jnp.float32(1), jnp.float32(0)
    )
    for c in range(0, n_vox, 8):
        before = jnp.zeros((8, VB), jnp.int32)
        for i in range(n_own):
            mark = turned(marks[c : c + 8, :], jnp.full((8, VB), i * n_vox + r, jnp.int32))
            for s in range(SLOTS):
                hit = (mark == 1) & (before == s)
                picks[i, s, c : c + 8, :] = jnp.where(hit, jnp.float32(1), jnp.float32(0))
            before = before + mark
    for i in range(n_own):
        totals = []
        for s in range(SLOTS):
            for half in range(2):
                total = None
                for c in range(half, n_vox, 2):
                    term = parts[c, s] * picks[i, s, c : c + 1, :]
                    total = term if total is None else total + term
                totals.append(total)
        out[i] = (totals[0] + totals[1]) + (totals[2] + totals[3])


def gram_kernel(*refs):
    received, (image, grams, parts) = refs[:-3], refs[-3:]
    n_frame, n_own, f_dev, _ = parts.shape
    own = lax.axis_index("frame")
    for flip in range(n_frame):
        parts[own ^ flip] = received[flip][...]
    spans = [
        jnp.concatenate([parts[f, i] for f in range(n_frame)], axis=0) for i in range(n_own)
    ]
    wide = jnp.concatenate(spans, axis=1)
    gram = dot(wide, wide, 1, 1)
    packed = jnp.concatenate([gram[f * f_dev : (f + 1) * f_dev] for f in range(n_frame)], axis=1)
    for i in range(grams.shape[0]):
        grams[i] = packed
    for f in range(n_frame):
        image[f * f_dev : (f + 1) * f_dev] = parts[f, own]


def orthonormal(columns):
    count = columns.shape[0]
    for k in range(count):
        current = columns[k]
        scale = lax.rsqrt(jnp.sum(current * current, axis=0, keepdims=True) + 1e-06)
        for j in range(k + 1, count):
            inner = jnp.sum(current * columns[j], axis=0, keepdims=True)
            columns[j] = columns[j] - (inner * (scale * scale)) * current
        columns[k] = current * scale


def subspace_kernel(grams, image, start, kept, out, square, columns):
    frames = image.shape[0]
    f_dev = grams.shape[1]
    count = columns.shape[0]
    packed = jnp.sum(grams[...], axis=0)
    for f in range(frames // f_dev):
        square[f * f_dev : (f + 1) * f_dev, :] = packed[:, f * frames : (f + 1) * frames]
    gram = square[...]
    for source in (start, columns):
        wide = dot(gram, jnp.concatenate([source[k] for k in range(count)], axis=1), 1, 0)
        for k in range(count):
            columns[k] = wide[:, k * VB : (k + 1) * VB]
        orthonormal(columns)
    own = image[...]
    left = own
    for k in range(count):
        coeffs = jnp.sum(columns[k] * own, axis=0, keepdims=True) * kept[k : k + 1, :]
        left = left - columns[k] * coeffs
    out[...] = left


def per_device(echoes, delays, apod, pattern, start_block, clutter_rank):
    n_vox = lax.axis_size("vox")
    n_frame = lax.axis_size("frame")
    f_dev, group, samples = echoes.shape
    frames = f_dev * n_frame
    n_blocks = delays.shape[0]
    n_own = n_blocks // n_vox
    n_tiles = samples // VB
    f32, i32 = jnp.float32, jnp.int32
    vmem = pl.BlockSpec(memory_space=pltpu.VMEM)
    smem = pl.BlockSpec(memory_space=pltpu.SMEM)
    hbm = pl.BlockSpec(memory_space=pltpu.HBM)
    params = pltpu.CompilerParams(vmem_limit_bytes=32 * 1024 * 1024)
    all_vmem = pltpu.CompilerParams(vmem_limit_bytes=56 * 1024 * 1024)
    slots = pl.pallas_call(
        beam_kernel,
        out_shape=jax.ShapeDtypeStruct((n_vox * SLOTS, f_dev, VB), f32),
        in_specs=[hbm, hbm, hbm, hbm],
        out_specs=vmem,
        scratch_shapes=[
            pltpu.VMEM((f_dev * group, samples), echoes.dtype),
            pltpu.VMEM(((n_tiles + 1) * group, f_dev, VB), f32),
            pltpu.VMEM((group, n_blocks), i32),
            pltpu.VMEM((group, n_blocks), apod.dtype),
            pltpu.SMEM((pattern.shape[1], n_blocks), i32),
            pltpu.VMEM((group, n_blocks), i32),
            pltpu.SMEM((group, n_blocks), i32),
            pltpu.VMEM((group, n_blocks), i32),
            pltpu.SMEM((group, n_blocks), i32),
            pltpu.VMEM((2 * STEP * group, VB), f32),
            pltpu.SMEM((n_vox * SLOTS + 3 * STEP,), i32),
            pltpu.SMEM((n_vox * SLOTS + 3 * STEP,), i32),
            pltpu.SemaphoreType.DMA((5,)),
            pltpu.SemaphoreType.DMA((f_dev,)),
        ],
        compiler_params=all_vmem,
    )(pattern.T, delays.T, apod.T, echoes)
    slots, later_rank, later_start = lax.optimization_barrier((slots, clutter_rank, start_block))
    wide_start = jnp.broadcast_to(later_start.T[:, :, None], (start_block.shape[1], frames, VB))
    parts = lax.all_to_all(slots, "vox", split_axis=0, concat_axis=0, tiled=True)
    placed, kept = pl.pallas_call(
        place_kernel,
        out_shape=(
            jax.ShapeDtypeStruct((n_own, f_dev, VB), f32),
            jax.ShapeDtypeStruct((start_block.shape[1], VB), f32),
        ),
        in_specs=[smem, vmem, vmem],
        out_specs=(vmem, vmem),
        scratch_shapes=[pltpu.VMEM((n_own, SLOTS, n_vox, VB), f32)],
        compiler_params=params,
    )(later_rank, pattern.T, parts.reshape(n_vox, SLOTS, f_dev, VB))

    def flipped(value, flip):
        return lax.ppermute(value, "frame", [(f, f ^ flip) for f in range(n_frame)])

    across = flipped(placed, 2)
    received = [placed, flipped(placed, 1), across, flipped(across, 1)]
    own_image, grams = pl.pallas_call(
        gram_kernel,
        out_shape=(
            jax.ShapeDtypeStruct((frames, VB), f32),
            jax.ShapeDtypeStruct((n_vox, f_dev, VB), f32),
        ),
        in_specs=[vmem] * n_frame,
        out_specs=(vmem, vmem),
        scratch_shapes=[pltpu.VMEM((n_frame, n_own, f_dev, VB), f32)],
        compiler_params=params,
    )(*received)
    grams = lax.all_to_all(grams, "vox", split_axis=0, concat_axis=0, tiled=True)
    return pl.pallas_call(
        subspace_kernel,
        out_shape=jax.ShapeDtypeStruct((frames, VB), f32),
        in_specs=[vmem, vmem, vmem, vmem],
        out_specs=vmem,
        scratch_shapes=[
            pltpu.VMEM((frames, frames), f32),
            pltpu.VMEM((start_block.shape[1], frames, VB), f32),
        ],
        compiler_params=params,
    )(grams, own_image, wide_start, kept)


def solution(mesh):
    placed = (P("frame", "vox", None), P(None, "vox"), P(None, "vox"), P(), P(), P())
    return jax.shard_map(
        per_device, mesh=mesh, in_specs=placed, out_specs=P(None, ("frame", "vox")), check_vma=False
    )
```

```python
import jax
import jax.numpy as jnp
from jax import lax
from jax.experimental import pallas as pl
from jax.experimental.pallas import tpu as pltpu
from jax.sharding import PartitionSpec as P

VB = 128
SLOTS = 2
STEP = 8
HIGHEST = lax.Precision.HIGHEST


def dot(a, b, da, db):
    return lax.dot_general(
        a, b, (((da,), (db,)), ((), ())), precision=HIGHEST, preferred_element_type=jnp.float32
    )


def turned(value, index):
    return jnp.take_along_axis(value, index, axis=1, mode="promise_in_bounds")


def beam_kernel(
    pattern_in, delays_in, apod_in, echoes_in, out,
    raw, tiles, delays, apod, marks, rows, row_words, turns, turn_words, weight_wide,
    blocks, places, sems, echo_sems,
):
    f_dev, group, samples = echoes_in.shape
    n_tiles = samples // VB
    tile_rows = group * f_dev
    n_blocks = marks.shape[1]
    n_vox = out.shape[0] // SLOTS
    n_own = n_blocks // n_vox
    column = lax.axis_index("vox")
    copy_delays = pltpu.make_async_copy(delays_in, delays, sems.at[0])
    copy_marks = pltpu.make_async_copy(pattern_in, marks, sems.at[1])
    copy_apod = pltpu.make_async_copy(apod_in, apod, sems.at[2])
    copy_delays.start()
    copy_marks.start()
    copies = []
    for part in range(2):
        own = pl.ds(part * (f_dev // 2), f_dev // 2)
        copies.append(pltpu.make_async_copy(echoes_in.at[own], raw.at[own], echo_sems.at[part]))
        copies[part].start()
    copy_apod.start()

    to_row = lax.broadcasted_iota(jnp.int32, (tile_rows, tile_rows), 0)
    from_row = lax.broadcasted_iota(jnp.int32, (tile_rows, tile_rows), 1)
    moves = (to_row & (f_dev - 1)) * group + lax.shift_right_logical(to_row, 3) == from_row
    moves = jnp.where(moves, 1.0, 0.0).astype(raw.dtype)
    tiles[0:group] = jnp.zeros((group, f_dev, VB), jnp.float32)

    copy_delays.wait()
    element = lax.broadcasted_iota(jnp.int32, delays.shape, 0)
    rows[...] = lax.shift_right_logical(delays[...] + (VB - 1), 7) * group + element
    turns[...] = (VB - (delays[...] & (VB - 1))) & (VB - 1)
    put_rows = pltpu.make_async_copy(rows, row_words, sems.at[3])
    put_turns = pltpu.make_async_copy(turns, turn_words, sems.at[4])
    put_rows.start()
    put_turns.start()

    copy_marks.wait()
    count = jnp.int32(0)
    for r in range(n_vox):
        first = jnp.int32(n_own)
        second = jnp.int32(n_own)
        for i in range(n_own - 1, -1, -1):
            marked = marks[column, i * n_vox + r] == 1
            second = jnp.where(marked, first, second)
            first = jnp.where(marked, i, first)
        blocks[count] = first * n_vox + r
        places[count] = r * SLOTS
        blocks[count + 1] = second * n_vox + r
        places[count + 1] = r * SLOTS + 1
        out[r * SLOTS + 1] = jnp.zeros(out.shape[1:], jnp.float32)
        count = count + jnp.where(second < n_own, 2, 1)
    for i in range(2 * STEP - 1):
        blocks[count + i] = blocks[count - 1]
        places[count + i] = places[count - 1]

    past = VB - lax.broadcasted_iota(jnp.int32, (f_dev, VB), 1)
    block_row = lax.broadcasted_iota(jnp.int32, (n_blocks, VB), 0)

    def spread(s, half):
        for i in range(STEP):
            pick = jnp.where(block_row == blocks[s * STEP + i], 1.0, 0.0).astype(apod.dtype)
            at = pl.ds((half * STEP + i) * group, group)
            weight_wide[at, :] = jnp.dot(apod[...], pick, preferred_element_type=jnp.float32)

    copy_apod.wait()
    spread(0, 0)
    for copy in copies:
        copy.wait()

    for q in range(0, n_tiles, 2):
        pair = raw[:, :, q * VB : (q + 2) * VB].reshape(tile_rows, 2 * VB)
        pair = jnp.dot(moves, pair, preferred_element_type=jnp.float32)
        for half in range(2):
            tiles[(q + half + 1) * group : (q + half + 2) * group] = pair[
                :, half * VB : (half + 1) * VB
            ].reshape(group, f_dev, VB)

    put_rows.wait()
    put_turns.wait()

    def step(s, carry):
        half = s & 1
        own = [blocks[s * STEP + i] for i in range(STEP)]
        totals = [None] * STEP
        for e in range(group):
            for i in range(STEP):
                row = row_words[e, own[i]]
                turn = turn_words[e, own[i]]
                mixed = jnp.where(past <= turn, tiles[row], tiles[row + group])
                weight = weight_wide[pl.ds((half * STEP + i) * group + e, 1), :]
                term = pltpu.roll(mixed, turn, 1) * weight
                totals[i] = term if e == 0 else totals[i] + term
        for i in range(STEP):
            out[places[s * STEP + i]] = totals[i]
        spread(s + 1, 1 - half)
        return carry

    lax.fori_loop(0, (count + STEP - 1) // STEP, step, 0)


def place_kernel(rank, marks, parts, out, kept, picks):
    n_vox = parts.shape[0]
    n_own = out.shape[0]
    r = lax.axis_index("vox")
    kept[...] = jnp.where(
        lax.broadcasted_iota(jnp.int32, kept.shape, 0) < rank[0], jnp.float32(1), jnp.float32(0)
    )
    for c in range(0, n_vox, 8):
        before = jnp.zeros((8, VB), jnp.int32)
        for i in range(n_own):
            mark = turned(marks[c : c + 8, :], jnp.full((8, VB), i * n_vox + r, jnp.int32))
            for s in range(SLOTS):
                hit = (mark == 1) & (before == s)
                picks[i, s, c : c + 8, :] = jnp.where(hit, jnp.float32(1), jnp.float32(0))
            before = before + mark
    for i in range(n_own):
        totals = []
        for s in range(SLOTS):
            for half in range(2):
                total = None
                for c in range(half, n_vox, 2):
                    term = parts[c, s] * picks[i, s, c : c + 1, :]
                    total = term if total is None else total + term
                totals.append(total)
        out[i] = (totals[0] + totals[1]) + (totals[2] + totals[3])


def gram_kernel(*refs):
    received, (image, grams, parts) = refs[:-3], refs[-3:]
    n_frame, n_own, f_dev, _ = parts.shape
    own = lax.axis_index("frame")
    for flip in range(n_frame):
        parts[own ^ flip] = received[flip][...]
    spans = [
        jnp.concatenate([parts[f, i] for f in range(n_frame)], axis=0) for i in range(n_own)
    ]
    wide = jnp.concatenate(spans, axis=1)
    gram = dot(wide, wide, 1, 1)
    packed = jnp.concatenate([gram[f * f_dev : (f + 1) * f_dev] for f in range(n_frame)], axis=1)
    for i in range(grams.shape[0]):
        grams[i] = packed
    for f in range(n_frame):
        image[f * f_dev : (f + 1) * f_dev] = parts[f, own]


def orthonormal(columns):
    count = columns.shape[0]
    for k in range(count):
        current = columns[k]
        scale = lax.rsqrt(jnp.sum(current * current, axis=0, keepdims=True) + 1e-06)
        for j in range(k + 1, count):
            inner = jnp.sum(current * columns[j], axis=0, keepdims=True)
            columns[j] = columns[j] - (inner * (scale * scale)) * current
        columns[k] = current * scale


def subspace_kernel(grams, image, start, kept, out, square, columns):
    frames = image.shape[0]
    f_dev = grams.shape[1]
    count = columns.shape[0]
    packed = jnp.sum(grams[...], axis=0)
    for f in range(frames // f_dev):
        square[f * f_dev : (f + 1) * f_dev, :] = packed[:, f * frames : (f + 1) * frames]
    gram = square[...]
    for source in (start, columns):
        wide = dot(gram, jnp.concatenate([source[k] for k in range(count)], axis=1), 1, 0)
        for k in range(count):
            columns[k] = wide[:, k * VB : (k + 1) * VB]
        orthonormal(columns)
    own = image[...]
    left = own
    for k in range(count):
        coeffs = jnp.sum(columns[k] * own, axis=0, keepdims=True) * kept[k : k + 1, :]
        left = left - columns[k] * coeffs
    out[...] = left


def per_device(echoes, delays, apod, pattern, start_block, clutter_rank):
    n_vox = lax.axis_size("vox")
    n_frame = lax.axis_size("frame")
    f_dev, group, samples = echoes.shape
    frames = f_dev * n_frame
    n_blocks = delays.shape[0]
    n_own = n_blocks // n_vox
    n_tiles = samples // VB
    f32, i32 = jnp.float32, jnp.int32
    vmem = pl.BlockSpec(memory_space=pltpu.VMEM)
    smem = pl.BlockSpec(memory_space=pltpu.SMEM)
    hbm = pl.BlockSpec(memory_space=pltpu.HBM)
    params = pltpu.CompilerParams(vmem_limit_bytes=32 * 1024 * 1024)
    all_vmem = pltpu.CompilerParams(vmem_limit_bytes=56 * 1024 * 1024)
    slots = pl.pallas_call(
        beam_kernel,
        out_shape=jax.ShapeDtypeStruct((n_vox * SLOTS, f_dev, VB), f32),
        in_specs=[hbm, hbm, hbm, hbm],
        out_specs=vmem,
        scratch_shapes=[
            pltpu.VMEM(echoes.shape, echoes.dtype),
            pltpu.VMEM(((n_tiles + 1) * group, f_dev, VB), f32),
            pltpu.VMEM((group, n_blocks), i32),
            pltpu.VMEM((group, n_blocks), apod.dtype),
            pltpu.SMEM((pattern.shape[1], n_blocks), i32),
            pltpu.VMEM((group, n_blocks), i32),
            pltpu.SMEM((group, n_blocks), i32),
            pltpu.VMEM((group, n_blocks), i32),
            pltpu.SMEM((group, n_blocks), i32),
            pltpu.VMEM((2 * STEP * group, VB), f32),
            pltpu.SMEM((n_vox * SLOTS + 3 * STEP,), i32),
            pltpu.SMEM((n_vox * SLOTS + 3 * STEP,), i32),
            pltpu.SemaphoreType.DMA((5,)),
            pltpu.SemaphoreType.DMA((2,)),
        ],
        compiler_params=all_vmem,
    )(pattern.T, delays.T, apod.T, echoes)
    slots, later_rank, later_start = lax.optimization_barrier((slots, clutter_rank, start_block))
    wide_start = jnp.broadcast_to(later_start.T[:, :, None], (start_block.shape[1], frames, VB))
    parts = lax.all_to_all(slots, "vox", split_axis=0, concat_axis=0, tiled=True)
    placed, kept = pl.pallas_call(
        place_kernel,
        out_shape=(
            jax.ShapeDtypeStruct((n_own, f_dev, VB), f32),
            jax.ShapeDtypeStruct((start_block.shape[1], VB), f32),
        ),
        in_specs=[smem, vmem, vmem],
        out_specs=(vmem, vmem),
        scratch_shapes=[pltpu.VMEM((n_own, SLOTS, n_vox, VB), f32)],
        compiler_params=params,
    )(later_rank, pattern.T, parts.reshape(n_vox, SLOTS, f_dev, VB))

    def flipped(value, flip):
        return lax.ppermute(value, "frame", [(f, f ^ flip) for f in range(n_frame)])

    across = flipped(placed, 2)
    received = [placed, flipped(placed, 1), across, flipped(across, 1)]
    own_image, grams = pl.pallas_call(
        gram_kernel,
        out_shape=(
            jax.ShapeDtypeStruct((frames, VB), f32),
            jax.ShapeDtypeStruct((n_vox, f_dev, VB), f32),
        ),
        in_specs=[vmem] * n_frame,
        out_specs=(vmem, vmem),
        scratch_shapes=[pltpu.VMEM((n_frame, n_own, f_dev, VB), f32)],
        compiler_params=params,
    )(*received)
    grams = lax.all_to_all(grams, "vox", split_axis=0, concat_axis=0, tiled=True)
    return pl.pallas_call(
        subspace_kernel,
        out_shape=jax.ShapeDtypeStruct((frames, VB), f32),
        in_specs=[vmem, vmem, vmem, vmem],
        out_specs=vmem,
        scratch_shapes=[
            pltpu.VMEM((frames, frames), f32),
            pltpu.VMEM((start_block.shape[1], frames, VB), f32),
        ],
        compiler_params=params,
    )(grams, own_image, wide_start, kept)


def solution(mesh):
    placed = (P("frame", "vox", None), P(None, "vox"), P(None, "vox"), P(), P(), P())
    return jax.shard_map(
        per_device, mesh=mesh, in_specs=placed, out_specs=P(None, ("frame", "vox")), check_vma=False
    )
```

```python
import jax
import jax.numpy as jnp
from jax import lax
from jax.experimental import pallas as pl
from jax.experimental.pallas import tpu as pltpu
from jax.sharding import PartitionSpec as P

VB = 128
SLOTS = 2
STEP = 8
HIGHEST = lax.Precision.HIGHEST


def dot(a, b, da, db):
    return lax.dot_general(
        a, b, (((da,), (db,)), ((), ())), precision=HIGHEST, preferred_element_type=jnp.float32
    )


def turned(value, index):
    return jnp.take_along_axis(value, index, axis=1, mode="promise_in_bounds")


def beam_kernel(
    pattern_in, delays_in, apod_in, echoes_in, out,
    raw, tiles, delays, apod, marks, rows, row_words, turns, turn_words, weight_wide,
    blocks, places, sems, echo_sems,
):
    f_dev, group, samples = echoes_in.shape
    n_tiles = samples // VB
    tile_rows = group * f_dev
    n_blocks = marks.shape[1]
    n_vox = out.shape[0] // SLOTS
    n_own = n_blocks // n_vox
    column = lax.axis_index("vox")
    near_row = lax.rem(column, 8)
    copy_delays = pltpu.make_async_copy(delays_in, delays, sems.at[0])
    near = pl.ds(pl.multiple_of((column // 8) * 8, 8), 8)
    copy_marks = pltpu.make_async_copy(pattern_in.at[near], marks, sems.at[1])
    copy_apod = pltpu.make_async_copy(apod_in, apod, sems.at[2])
    copy_delays.start()
    copy_marks.start()
    copies = []
    for part in range(2):
        own = pl.ds(part * (f_dev // 2), f_dev // 2)
        copies.append(pltpu.make_async_copy(echoes_in.at[own], raw.at[own], echo_sems.at[part]))
        copies[part].start()
    copy_apod.start()

    to_row = lax.broadcasted_iota(jnp.int32, (tile_rows, tile_rows), 0)
    from_row = lax.broadcasted_iota(jnp.int32, (tile_rows, tile_rows), 1)
    moves = (to_row & (f_dev - 1)) * group + lax.shift_right_logical(to_row, 3) == from_row
    moves = jnp.where(moves, 1.0, 0.0).astype(raw.dtype)
    tiles[0:group] = jnp.zeros((group, f_dev, VB), jnp.float32)

    copy_delays.wait()
    element = lax.broadcasted_iota(jnp.int32, delays.shape, 0)
    rows[...] = lax.shift_right_logical(delays[...] + (VB - 1), 7) * group + element
    turns[...] = (VB - (delays[...] & (VB - 1))) & (VB - 1)
    put_rows = pltpu.make_async_copy(rows, row_words, sems.at[3])
    put_turns = pltpu.make_async_copy(turns, turn_words, sems.at[4])
    put_rows.start()
    put_turns.start()

    for copy in copies:
        copy.wait()

    for q in range(0, n_tiles, 2):
        pair = raw[:, :, q * VB : (q + 2) * VB].reshape(tile_rows, 2 * VB)
        pair = jnp.dot(moves, pair, preferred_element_type=jnp.float32)
        for half in range(2):
            tiles[(q + half + 1) * group : (q + half + 2) * group] = pair[
                :, half * VB : (half + 1) * VB
            ].reshape(group, f_dev, VB)

    copy_marks.wait()
    count = jnp.int32(0)
    for r in range(n_vox):
        first = jnp.int32(n_own)
        second = jnp.int32(n_own)
        for i in range(n_own - 1, -1, -1):
            marked = marks[near_row, i * n_vox + r] == 1
            second = jnp.where(marked, first, second)
            first = jnp.where(marked, i, first)
        blocks[count] = first * n_vox + r
        places[count] = r * SLOTS
        blocks[count + 1] = second * n_vox + r
        places[count + 1] = r * SLOTS + 1
        out[r * SLOTS + 1] = jnp.zeros(out.shape[1:], jnp.float32)
        count = count + jnp.where(second < n_own, 2, 1)
    for i in range(2 * STEP - 1):
        blocks[count + i] = blocks[count - 1]
        places[count + i] = places[count - 1]

    past = VB - lax.broadcasted_iota(jnp.int32, (f_dev, VB), 1)
    block_row = lax.broadcasted_iota(jnp.int32, (n_blocks, VB), 0)

    def spread(s, half):
        for i in range(STEP):
            pick = jnp.where(block_row == blocks[s * STEP + i], 1.0, 0.0).astype(apod.dtype)
            at = pl.ds((half * STEP + i) * group, group)
            weight_wide[at, :] = jnp.dot(apod[...], pick, preferred_element_type=jnp.float32)

    copy_apod.wait()
    spread(0, 0)
    put_rows.wait()
    put_turns.wait()

    def step(s, carry):
        half = s & 1
        own = [blocks[s * STEP + i] for i in range(STEP)]
        totals = [None] * STEP
        for e in range(group):
            for i in range(STEP):
                row = row_words[e, own[i]]
                turn = turn_words[e, own[i]]
                mixed = jnp.where(past <= turn, tiles[row], tiles[row + group])
                weight = weight_wide[pl.ds((half * STEP + i) * group + e, 1), :]
                term = pltpu.roll(mixed, turn, 1) * weight
                totals[i] = term if e == 0 else totals[i] + term
        for i in range(STEP):
            out[places[s * STEP + i]] = totals[i]
        spread(s + 1, 1 - half)
        return carry

    lax.fori_loop(0, (count + STEP - 1) // STEP, step, 0)


def place_kernel(rank, marks, parts, out, kept, picks):
    n_vox = parts.shape[0]
    n_own = out.shape[0]
    r = lax.axis_index("vox")
    kept[...] = jnp.where(
        lax.broadcasted_iota(jnp.int32, kept.shape, 0) < rank[0], jnp.float32(1), jnp.float32(0)
    )
    for c in range(0, n_vox, 8):
        before = jnp.zeros((8, VB), jnp.int32)
        for i in range(n_own):
            mark = turned(marks[c : c + 8, :], jnp.full((8, VB), i * n_vox + r, jnp.int32))
            for s in range(SLOTS):
                hit = (mark == 1) & (before == s)
                picks[i, s, c : c + 8, :] = jnp.where(hit, jnp.float32(1), jnp.float32(0))
            before = before + mark
    for i in range(n_own):
        totals = []
        for s in range(SLOTS):
            for half in range(2):
                total = None
                for c in range(half, n_vox, 2):
                    term = parts[c, s] * picks[i, s, c : c + 1, :]
                    total = term if total is None else total + term
                totals.append(total)
        out[i] = (totals[0] + totals[1]) + (totals[2] + totals[3])


def gram_kernel(*refs):
    received, (image, grams, parts) = refs[:-3], refs[-3:]
    n_frame, n_own, f_dev, _ = parts.shape
    own = lax.axis_index("frame")
    for flip in range(n_frame):
        parts[own ^ flip] = received[flip][...]
    spans = [
        jnp.concatenate([parts[f, i] for f in range(n_frame)], axis=0) for i in range(n_own)
    ]
    wide = jnp.concatenate(spans, axis=1)
    gram = dot(wide, wide, 1, 1)
    packed = jnp.concatenate([gram[f * f_dev : (f + 1) * f_dev] for f in range(n_frame)], axis=1)
    for i in range(grams.shape[0]):
        grams[i] = packed
    for f in range(n_frame):
        image[f * f_dev : (f + 1) * f_dev] = parts[f, own]


def orthonormal(columns):
    count = columns.shape[0]
    for k in range(count):
        current = columns[k]
        scale = lax.rsqrt(jnp.sum(current * current, axis=0, keepdims=True) + 1e-06)
        for j in range(k + 1, count):
            inner = jnp.sum(current * columns[j], axis=0, keepdims=True)
            columns[j] = columns[j] - (inner * (scale * scale)) * current
        columns[k] = current * scale


def subspace_kernel(grams, image, start, kept, out, square, columns):
    frames = image.shape[0]
    f_dev = grams.shape[1]
    count = columns.shape[0]
    packed = jnp.sum(grams[...], axis=0)
    for f in range(frames // f_dev):
        square[f * f_dev : (f + 1) * f_dev, :] = packed[:, f * frames : (f + 1) * frames]
    gram = square[...]
    for source in (start, columns):
        wide = dot(gram, jnp.concatenate([source[k] for k in range(count)], axis=1), 1, 0)
        for k in range(count):
            columns[k] = wide[:, k * VB : (k + 1) * VB]
        orthonormal(columns)
    own = image[...]
    left = own
    for k in range(count):
        coeffs = jnp.sum(columns[k] * own, axis=0, keepdims=True) * kept[k : k + 1, :]
        left = left - columns[k] * coeffs
    out[...] = left


def per_device(echoes, delays, apod, pattern, start_block, clutter_rank):
    n_vox = lax.axis_size("vox")
    n_frame = lax.axis_size("frame")
    f_dev, group, samples = echoes.shape
    frames = f_dev * n_frame
    n_blocks = delays.shape[0]
    n_own = n_blocks // n_vox
    n_tiles = samples // VB
    f32, i32 = jnp.float32, jnp.int32
    vmem = pl.BlockSpec(memory_space=pltpu.VMEM)
    smem = pl.BlockSpec(memory_space=pltpu.SMEM)
    hbm = pl.BlockSpec(memory_space=pltpu.HBM)
    params = pltpu.CompilerParams(vmem_limit_bytes=32 * 1024 * 1024)
    all_vmem = pltpu.CompilerParams(vmem_limit_bytes=56 * 1024 * 1024)
    slots = pl.pallas_call(
        beam_kernel,
        out_shape=jax.ShapeDtypeStruct((n_vox * SLOTS, f_dev, VB), f32),
        in_specs=[hbm, hbm, hbm, hbm],
        out_specs=vmem,
        scratch_shapes=[
            pltpu.VMEM(echoes.shape, echoes.dtype),
            pltpu.VMEM(((n_tiles + 1) * group, f_dev, VB), f32),
            pltpu.VMEM((group, n_blocks), i32),
            pltpu.VMEM((group, n_blocks), apod.dtype),
            pltpu.SMEM((8, n_blocks), i32),
            pltpu.VMEM((group, n_blocks), i32),
            pltpu.SMEM((group, n_blocks), i32),
            pltpu.VMEM((group, n_blocks), i32),
            pltpu.SMEM((group, n_blocks), i32),
            pltpu.VMEM((2 * STEP * group, VB), f32),
            pltpu.SMEM((n_vox * SLOTS + 3 * STEP,), i32),
            pltpu.SMEM((n_vox * SLOTS + 3 * STEP,), i32),
            pltpu.SemaphoreType.DMA((5,)),
            pltpu.SemaphoreType.DMA((2,)),
        ],
        compiler_params=all_vmem,
    )(pattern.T, delays.T, apod.T, echoes)
    slots, later_rank, later_start = lax.optimization_barrier((slots, clutter_rank, start_block))
    wide_start = jnp.broadcast_to(later_start.T[:, :, None], (start_block.shape[1], frames, VB))
    parts = lax.all_to_all(slots, "vox", split_axis=0, concat_axis=0, tiled=True)
    placed, kept = pl.pallas_call(
        place_kernel,
        out_shape=(
            jax.ShapeDtypeStruct((n_own, f_dev, VB), f32),
            jax.ShapeDtypeStruct((start_block.shape[1], VB), f32),
        ),
        in_specs=[smem, vmem, vmem],
        out_specs=(vmem, vmem),
        scratch_shapes=[pltpu.VMEM((n_own, SLOTS, n_vox, VB), f32)],
        compiler_params=params,
    )(later_rank, pattern.T, parts.reshape(n_vox, SLOTS, f_dev, VB))

    def flipped(value, flip):
        return lax.ppermute(value, "frame", [(f, f ^ flip) for f in range(n_frame)])

    across = flipped(placed, 2)
    received = [placed, flipped(placed, 1), across, flipped(across, 1)]
    own_image, grams = pl.pallas_call(
        gram_kernel,
        out_shape=(
            jax.ShapeDtypeStruct((frames, VB), f32),
            jax.ShapeDtypeStruct((n_vox, f_dev, VB), f32),
        ),
        in_specs=[vmem] * n_frame,
        out_specs=(vmem, vmem),
        scratch_shapes=[pltpu.VMEM((n_frame, n_own, f_dev, VB), f32)],
        compiler_params=params,
    )(*received)
    grams = lax.all_to_all(grams, "vox", split_axis=0, concat_axis=0, tiled=True)
    return pl.pallas_call(
        subspace_kernel,
        out_shape=jax.ShapeDtypeStruct((frames, VB), f32),
        in_specs=[vmem, vmem, vmem, vmem],
        out_specs=vmem,
        scratch_shapes=[
            pltpu.VMEM((frames, frames), f32),
            pltpu.VMEM((start_block.shape[1], frames, VB), f32),
        ],
        compiler_params=params,
    )(grams, own_image, wide_start, kept)


def solution(mesh):
    placed = (P("frame", "vox", None), P(None, "vox"), P(None, "vox"), P(), P(), P())
    return jax.shard_map(
        per_device, mesh=mesh, in_specs=placed, out_specs=P(None, ("frame", "vox")), check_vma=False
    )
```

```python
import jax
import jax.numpy as jnp
from jax import lax
from jax.experimental import pallas as pl
from jax.experimental.pallas import tpu as pltpu
from jax.sharding import PartitionSpec as P

VB = 128
SLOTS = 2
STEP = 8
REST = 2
HIGHEST = lax.Precision.HIGHEST


def dot(a, b, da, db):
    return lax.dot_general(
        a, b, (((da,), (db,)), ((), ())), precision=HIGHEST, preferred_element_type=jnp.float32
    )


def turned(value, index):
    return jnp.take_along_axis(value, index, axis=1, mode="promise_in_bounds")


def beam_kernel(
    pattern_in, delays_in, apod_in, echoes_in, out,
    raw, tiles, delays, apod, marks, rows, row_words, turns, turn_words, weight_wide,
    blocks, places, sems, echo_sems,
):
    f_dev, group, samples = echoes_in.shape
    n_tiles = samples // VB
    tile_rows = group * f_dev
    n_blocks = marks.shape[1]
    n_vox = out.shape[0] // SLOTS
    n_own = n_blocks // n_vox
    column = lax.axis_index("vox")
    copy_delays = pltpu.make_async_copy(delays_in, delays, sems.at[0])
    copy_marks = pltpu.make_async_copy(pattern_in, marks, sems.at[1])
    copy_apod = pltpu.make_async_copy(apod_in, apod, sems.at[2])
    copy_delays.start()
    copy_marks.start()
    copies = []
    for part in range(2):
        own = pl.ds(part * (f_dev // 2), f_dev // 2)
        copies.append(pltpu.make_async_copy(echoes_in.at[own], raw.at[own], echo_sems.at[part]))
        copies[part].start()
    copy_apod.start()

    tiles[0:group] = jnp.zeros((group, f_dev, VB), jnp.float32)

    copy_delays.wait()
    element = lax.broadcasted_iota(jnp.int32, delays.shape, 0)
    rows[...] = lax.shift_right_logical(delays[...] + (VB - 1), 7) * group + element
    turns[...] = (VB - (delays[...] & (VB - 1))) & (VB - 1)
    put_rows = pltpu.make_async_copy(rows, row_words, sems.at[3])
    put_turns = pltpu.make_async_copy(turns, turn_words, sems.at[4])
    put_rows.start()
    put_turns.start()

    copy_marks.wait()
    count = jnp.int32(0)
    for r in range(n_vox):
        first = jnp.int32(n_own)
        second = jnp.int32(n_own)
        for i in range(n_own - 1, -1, -1):
            marked = marks[column, i * n_vox + r] == 1
            second = jnp.where(marked, first, second)
            first = jnp.where(marked, i, first)
        blocks[count] = first * n_vox + r
        places[count] = r * SLOTS
        blocks[count + 1] = second * n_vox + r
        places[count + 1] = r * SLOTS + 1
        out[r * SLOTS + 1] = jnp.zeros(out.shape[1:], jnp.float32)
        count = count + jnp.where(second < n_own, 2, 1)
    for i in range(2 * STEP - 1):
        blocks[count + i] = blocks[count - 1]
        places[count + i] = places[count - 1]

    past = VB - lax.broadcasted_iota(jnp.int32, (f_dev, VB), 1)
    block_row = lax.broadcasted_iota(jnp.int32, (n_blocks, VB), 0)

    def spread(s, half):
        for i in range(STEP):
            pick = jnp.where(block_row == blocks[s * STEP + i], 1.0, 0.0).astype(apod.dtype)
            at = pl.ds((half * STEP + i) * group, group)
            weight_wide[at, :] = jnp.dot(apod[...], pick, preferred_element_type=jnp.float32)

    copy_apod.wait()
    spread(0, 0)
    for copy in copies:
        copy.wait()

    flat = tiles.reshape((n_tiles + 1) * tile_rows, VB)
    for q in range(n_tiles):
        for f in range(f_dev):
            flat[pl.ds((q + 1) * tile_rows + f, group, stride=f_dev), :] = raw[
                f, :, q * VB : (q + 1) * VB
            ].astype(jnp.float32)

    put_rows.wait()
    put_turns.wait()

    def beam(base, size):
        own = [blocks[base + i] for i in range(size)]
        at = (base & (2 * STEP - 1)) * group
        totals = [None] * size
        for e in range(group):
            for i in range(size):
                row = row_words[e, own[i]]
                turn = turn_words[e, own[i]]
                mixed = jnp.where(past <= turn, tiles[row], tiles[row + group])
                weight = weight_wide[pl.ds(at + i * group + e, 1), :]
                term = pltpu.roll(mixed, turn, 1) * weight
                totals[i] = term if e == 0 else totals[i] + term
        for i in range(size):
            out[places[base + i]] = totals[i]

    def full_step(s, carry):
        beam(s * STEP, STEP)
        spread(s + 1, 1 - (s & 1))
        return carry

    def rest_step(t, carry):
        beam(full * STEP + t * REST, REST)
        return carry

    full = count // STEP
    lax.fori_loop(0, full, full_step, 0)
    lax.fori_loop(0, (count - full * STEP + REST - 1) // REST, rest_step, 0)


def place_kernel(rank, marks, parts, out, kept, picks):
    n_vox = parts.shape[0]
    n_own = out.shape[0]
    r = lax.axis_index("vox")
    kept[...] = jnp.where(
        lax.broadcasted_iota(jnp.int32, kept.shape, 0) < rank[0], jnp.float32(1), jnp.float32(0)
    )
    for c in range(0, n_vox, 8):
        before = jnp.zeros((8, VB), jnp.int32)
        for i in range(n_own):
            mark = turned(marks[c : c + 8, :], jnp.full((8, VB), i * n_vox + r, jnp.int32))
            for s in range(SLOTS):
                hit = (mark == 1) & (before == s)
                picks[i, s, c : c + 8, :] = jnp.where(hit, jnp.float32(1), jnp.float32(0))
            before = before + mark
    for i in range(n_own):
        totals = []
        for s in range(SLOTS):
            for half in range(2):
                total = None
                for c in range(half, n_vox, 2):
                    term = parts[c, s] * picks[i, s, c : c + 1, :]
                    total = term if total is None else total + term
                totals.append(total)
        out[i] = (totals[0] + totals[1]) + (totals[2] + totals[3])


def gram_kernel(*refs):
    received, (image, grams, parts) = refs[:-3], refs[-3:]
    n_frame, n_own, f_dev, _ = parts.shape
    own = lax.axis_index("frame")
    for flip in range(n_frame):
        parts[own ^ flip] = received[flip][...]
    spans = [
        jnp.concatenate([parts[f, i] for f in range(n_frame)], axis=0) for i in range(n_own)
    ]
    wide = jnp.concatenate(spans, axis=1)
    gram = dot(wide, wide, 1, 1)
    packed = jnp.concatenate([gram[f * f_dev : (f + 1) * f_dev] for f in range(n_frame)], axis=1)
    for i in range(grams.shape[0]):
        grams[i] = packed
    for f in range(n_frame):
        image[f * f_dev : (f + 1) * f_dev] = parts[f, own]


def orthonormal(columns):
    count = columns.shape[0]
    for k in range(count):
        current = columns[k]
        scale = lax.rsqrt(jnp.sum(current * current, axis=0, keepdims=True) + 1e-06)
        for j in range(k + 1, count):
            inner = jnp.sum(current * columns[j], axis=0, keepdims=True)
            columns[j] = columns[j] - (inner * (scale * scale)) * current
        columns[k] = current * scale


def subspace_kernel(grams, image, start, kept, out, square, columns):
    frames = image.shape[0]
    f_dev = grams.shape[1]
    count = columns.shape[0]
    packed = jnp.sum(grams[...], axis=0)
    for f in range(frames // f_dev):
        square[f * f_dev : (f + 1) * f_dev, :] = packed[:, f * frames : (f + 1) * frames]
    gram = square[...]
    for source in (start, columns):
        wide = dot(gram, jnp.concatenate([source[k] for k in range(count)], axis=1), 1, 0)
        for k in range(count):
            columns[k] = wide[:, k * VB : (k + 1) * VB]
        orthonormal(columns)
    own = image[...]
    left = own
    for k in range(count):
        coeffs = jnp.sum(columns[k] * own, axis=0, keepdims=True) * kept[k : k + 1, :]
        left = left - columns[k] * coeffs
    out[...] = left


def per_device(echoes, delays, apod, pattern, start_block, clutter_rank):
    n_vox = lax.axis_size("vox")
    n_frame = lax.axis_size("frame")
    f_dev, group, samples = echoes.shape
    frames = f_dev * n_frame
    n_blocks = delays.shape[0]
    n_own = n_blocks // n_vox
    n_tiles = samples // VB
    f32, i32 = jnp.float32, jnp.int32
    vmem = pl.BlockSpec(memory_space=pltpu.VMEM)
    smem = pl.BlockSpec(memory_space=pltpu.SMEM)
    hbm = pl.BlockSpec(memory_space=pltpu.HBM)
    params = pltpu.CompilerParams(vmem_limit_bytes=32 * 1024 * 1024)
    all_vmem = pltpu.CompilerParams(vmem_limit_bytes=56 * 1024 * 1024)
    slots = pl.pallas_call(
        beam_kernel,
        out_shape=jax.ShapeDtypeStruct((n_vox * SLOTS, f_dev, VB), f32),
        in_specs=[hbm, hbm, hbm, hbm],
        out_specs=vmem,
        scratch_shapes=[
            pltpu.VMEM(echoes.shape, echoes.dtype),
            pltpu.VMEM(((n_tiles + 1) * group, f_dev, VB), f32),
            pltpu.VMEM((group, n_blocks), i32),
            pltpu.VMEM((group, n_blocks), apod.dtype),
            pltpu.SMEM((pattern.shape[1], n_blocks), i32),
            pltpu.VMEM((group, n_blocks), i32),
            pltpu.SMEM((group, n_blocks), i32),
            pltpu.VMEM((group, n_blocks), i32),
            pltpu.SMEM((group, n_blocks), i32),
            pltpu.VMEM((2 * STEP * group, VB), f32),
            pltpu.SMEM((n_vox * SLOTS + 3 * STEP,), i32),
            pltpu.SMEM((n_vox * SLOTS + 3 * STEP,), i32),
            pltpu.SemaphoreType.DMA((5,)),
            pltpu.SemaphoreType.DMA((2,)),
        ],
        compiler_params=all_vmem,
    )(pattern.T, delays.T, apod.T, echoes)
    slots, later_rank, later_start = lax.optimization_barrier((slots, clutter_rank, start_block))
    wide_start = jnp.broadcast_to(later_start.T[:, :, None], (start_block.shape[1], frames, VB))
    parts = lax.all_to_all(slots, "vox", split_axis=0, concat_axis=0, tiled=True)
    placed, kept = pl.pallas_call(
        place_kernel,
        out_shape=(
            jax.ShapeDtypeStruct((n_own, f_dev, VB), f32),
            jax.ShapeDtypeStruct((start_block.shape[1], VB), f32),
        ),
        in_specs=[smem, vmem, vmem],
        out_specs=(vmem, vmem),
        scratch_shapes=[pltpu.VMEM((n_own, SLOTS, n_vox, VB), f32)],
        compiler_params=params,
    )(later_rank, pattern.T, parts.reshape(n_vox, SLOTS, f_dev, VB))

    def flipped(value, flip):
        return lax.ppermute(value, "frame", [(f, f ^ flip) for f in range(n_frame)])

    across = flipped(placed, 2)
    received = [placed, flipped(placed, 1), across, flipped(across, 1)]
    own_image, grams = pl.pallas_call(
        gram_kernel,
        out_shape=(
            jax.ShapeDtypeStruct((frames, VB), f32),
            jax.ShapeDtypeStruct((n_vox, f_dev, VB), f32),
        ),
        in_specs=[vmem] * n_frame,
        out_specs=(vmem, vmem),
        scratch_shapes=[pltpu.VMEM((n_frame, n_own, f_dev, VB), f32)],
        compiler_params=params,
    )(*received)
    grams = lax.all_to_all(grams, "vox", split_axis=0, concat_axis=0, tiled=True)
    return pl.pallas_call(
        subspace_kernel,
        out_shape=jax.ShapeDtypeStruct((frames, VB), f32),
        in_specs=[vmem, vmem, vmem, vmem],
        out_specs=vmem,
        scratch_shapes=[
            pltpu.VMEM((frames, frames), f32),
            pltpu.VMEM((start_block.shape[1], frames, VB), f32),
        ],
        compiler_params=params,
    )(grams, own_image, wide_start, kept)


def solution(mesh):
    placed = (P("frame", "vox", None), P(None, "vox"), P(None, "vox"), P(), P(), P())
    return jax.shard_map(
        per_device, mesh=mesh, in_specs=placed, out_specs=P(None, ("frame", "vox")), check_vma=False
    )
```

```python
import jax
import jax.numpy as jnp
from jax import lax
from jax.experimental import pallas as pl
from jax.experimental.pallas import tpu as pltpu
from jax.sharding import PartitionSpec as P

VB = 128
SLOTS = 2
STEP = 8
REST = 2
HIGHEST = lax.Precision.HIGHEST


def dot(a, b, da, db):
    return lax.dot_general(
        a, b, (((da,), (db,)), ((), ())), precision=HIGHEST, preferred_element_type=jnp.float32
    )


def turned(value, index):
    return jnp.take_along_axis(value, index, axis=1, mode="promise_in_bounds")


def beam_kernel(
    pattern_in, delays_in, apod_in, echoes_in, out,
    raw, tiles, delays, apod, marks, rows, row_words, turns, turn_words, weight_wide,
    blocks, places, sems, echo_sems,
):
    f_dev, group, samples = echoes_in.shape
    n_tiles = samples // VB
    tile_rows = group * f_dev
    n_blocks = marks.shape[1]
    n_vox = out.shape[0] // SLOTS
    n_own = n_blocks // n_vox
    column = lax.axis_index("vox")
    copy_delays = pltpu.make_async_copy(delays_in, delays, sems.at[0])
    copy_marks = pltpu.make_async_copy(pattern_in, marks, sems.at[1])
    copy_apod = pltpu.make_async_copy(apod_in, apod, sems.at[2])
    copy_delays.start()
    copy_marks.start()
    copies = []
    for part in range(2):
        own = pl.ds(part * (f_dev // 2), f_dev // 2)
        copies.append(pltpu.make_async_copy(echoes_in.at[own], raw.at[own], echo_sems.at[part]))
        copies[part].start()
    copy_apod.start()

    tiles[0:group] = jnp.zeros((group, f_dev, VB), jnp.float32)

    copy_delays.wait()
    element = lax.broadcasted_iota(jnp.int32, delays.shape, 0)
    rows[...] = lax.shift_right_logical(delays[...] + (VB - 1), 7) * group + element
    turns[...] = (VB - (delays[...] & (VB - 1))) & (VB - 1)
    put_rows = pltpu.make_async_copy(rows, row_words, sems.at[3])
    put_turns = pltpu.make_async_copy(turns, turn_words, sems.at[4])
    put_rows.start()
    put_turns.start()

    copy_marks.wait()
    count = jnp.int32(0)
    for r in range(n_vox):
        first = jnp.int32(n_own)
        second = jnp.int32(n_own)
        for i in range(n_own - 1, -1, -1):
            marked = marks[column, i * n_vox + r] == 1
            second = jnp.where(marked, first, second)
            first = jnp.where(marked, i, first)
        blocks[count] = first * n_vox + r
        places[count] = r * SLOTS
        blocks[count + 1] = second * n_vox + r
        places[count + 1] = r * SLOTS + 1
        out[r * SLOTS + 1] = jnp.zeros(out.shape[1:], jnp.float32)
        count = count + jnp.where(second < n_own, 2, 1)
    for i in range(2 * STEP - 1):
        blocks[count + i] = blocks[count - 1]
        places[count + i] = places[count - 1]

    lane = lax.broadcasted_iota(jnp.int32, (f_dev, VB), 1)
    past = VB - lane
    block_row = lax.broadcasted_iota(jnp.int32, (n_blocks, VB), 0)

    def spread(s, half):
        for i in range(STEP):
            pick = jnp.where(block_row == blocks[s * STEP + i], 1.0, 0.0).astype(apod.dtype)
            at = pl.ds((half * STEP + i) * group, group)
            weight_wide[at, :] = jnp.dot(apod[...], pick, preferred_element_type=jnp.float32)

    copy_apod.wait()
    spread(0, 0)
    for copy in copies:
        copy.wait()

    flat = tiles.reshape((n_tiles + 1) * tile_rows, VB)
    for q in range(n_tiles):
        for f in range(f_dev):
            flat[pl.ds((q + 1) * tile_rows + f, group, stride=f_dev), :] = raw[
                f, :, q * VB : (q + 1) * VB
            ].astype(jnp.float32)

    put_rows.wait()
    put_turns.wait()

    def beam(base, size):
        own = [blocks[base + i] for i in range(size)]
        at = (base & (2 * STEP - 1)) * group
        totals = [None] * size
        for e in range(group):
            for i in range(size):
                row = row_words[e, own[i]]
                turn = turn_words[e, own[i]]
                mixed = jnp.where(past <= turn, tiles[row], tiles[row + group])
                weight = weight_wide[pl.ds(at + i * group + e, 1), :]
                if e % 4 == 3:
                    term = turned(mixed, (lane - turn) & (VB - 1)) * weight
                else:
                    term = pltpu.roll(mixed, turn, 1) * weight
                totals[i] = term if e == 0 else totals[i] + term
        for i in range(size):
            out[places[base + i]] = totals[i]

    def full_step(s, carry):
        beam(s * STEP, STEP)
        spread(s + 1, 1 - (s & 1))
        return carry

    def rest_step(t, carry):
        beam(full * STEP + t * REST, REST)
        return carry

    full = count // STEP
    lax.fori_loop(0, full, full_step, 0)
    lax.fori_loop(0, (count - full * STEP + REST - 1) // REST, rest_step, 0)


def place_kernel(rank, marks, parts, out, kept, picks):
    n_vox = parts.shape[0]
    n_own = out.shape[0]
    r = lax.axis_index("vox")
    kept[...] = jnp.where(
        lax.broadcasted_iota(jnp.int32, kept.shape, 0) < rank[0], jnp.float32(1), jnp.float32(0)
    )
    for c in range(0, n_vox, 8):
        before = jnp.zeros((8, VB), jnp.int32)
        for i in range(n_own):
            mark = turned(marks[c : c + 8, :], jnp.full((8, VB), i * n_vox + r, jnp.int32))
            for s in range(SLOTS):
                hit = (mark == 1) & (before == s)
                picks[i, s, c : c + 8, :] = jnp.where(hit, jnp.float32(1), jnp.float32(0))
            before = before + mark
    for i in range(n_own):
        totals = []
        for s in range(SLOTS):
            for half in range(2):
                total = None
                for c in range(half, n_vox, 2):
                    term = parts[c, s] * picks[i, s, c : c + 1, :]
                    total = term if total is None else total + term
                totals.append(total)
        out[i] = (totals[0] + totals[1]) + (totals[2] + totals[3])


def gram_kernel(*refs):
    received, (image, grams, parts) = refs[:-3], refs[-3:]
    n_frame, n_own, f_dev, _ = parts.shape
    own = lax.axis_index("frame")
    for flip in range(n_frame):
        parts[own ^ flip] = received[flip][...]
    spans = [
        jnp.concatenate([parts[f, i] for f in range(n_frame)], axis=0) for i in range(n_own)
    ]
    wide = jnp.concatenate(spans, axis=1)
    gram = dot(wide, wide, 1, 1)
    packed = jnp.concatenate([gram[f * f_dev : (f + 1) * f_dev] for f in range(n_frame)], axis=1)
    for i in range(grams.shape[0]):
        grams[i] = packed
    for f in range(n_frame):
        image[f * f_dev : (f + 1) * f_dev] = parts[f, own]


def orthonormal(columns):
    count = columns.shape[0]
    for k in range(count):
        current = columns[k]
        scale = lax.rsqrt(jnp.sum(current * current, axis=0, keepdims=True) + 1e-06)
        for j in range(k + 1, count):
            inner = jnp.sum(current * columns[j], axis=0, keepdims=True)
            columns[j] = columns[j] - (inner * (scale * scale)) * current
        columns[k] = current * scale


def subspace_kernel(grams, image, start, kept, out, square, columns):
    frames = image.shape[0]
    f_dev = grams.shape[1]
    count = columns.shape[0]
    packed = jnp.sum(grams[...], axis=0)
    for f in range(frames // f_dev):
        square[f * f_dev : (f + 1) * f_dev, :] = packed[:, f * frames : (f + 1) * frames]
    gram = square[...]
    for source in (start, columns):
        wide = dot(gram, jnp.concatenate([source[k] for k in range(count)], axis=1), 1, 0)
        for k in range(count):
            columns[k] = wide[:, k * VB : (k + 1) * VB]
        orthonormal(columns)
    own = image[...]
    left = own
    for k in range(count):
        coeffs = jnp.sum(columns[k] * own, axis=0, keepdims=True) * kept[k : k + 1, :]
        left = left - columns[k] * coeffs
    out[...] = left


def per_device(echoes, delays, apod, pattern, start_block, clutter_rank):
    n_vox = lax.axis_size("vox")
    n_frame = lax.axis_size("frame")
    f_dev, group, samples = echoes.shape
    frames = f_dev * n_frame
    n_blocks = delays.shape[0]
    n_own = n_blocks // n_vox
    n_tiles = samples // VB
    f32, i32 = jnp.float32, jnp.int32
    vmem = pl.BlockSpec(memory_space=pltpu.VMEM)
    smem = pl.BlockSpec(memory_space=pltpu.SMEM)
    hbm = pl.BlockSpec(memory_space=pltpu.HBM)
    params = pltpu.CompilerParams(vmem_limit_bytes=32 * 1024 * 1024)
    all_vmem = pltpu.CompilerParams(vmem_limit_bytes=56 * 1024 * 1024)
    slots = pl.pallas_call(
        beam_kernel,
        out_shape=jax.ShapeDtypeStruct((n_vox * SLOTS, f_dev, VB), f32),
        in_specs=[hbm, hbm, hbm, hbm],
        out_specs=vmem,
        scratch_shapes=[
            pltpu.VMEM(echoes.shape, echoes.dtype),
            pltpu.VMEM(((n_tiles + 1) * group, f_dev, VB), f32),
            pltpu.VMEM((group, n_blocks), i32),
            pltpu.VMEM((group, n_blocks), apod.dtype),
            pltpu.SMEM((pattern.shape[1], n_blocks), i32),
            pltpu.VMEM((group, n_blocks), i32),
            pltpu.SMEM((group, n_blocks), i32),
            pltpu.VMEM((group, n_blocks), i32),
            pltpu.SMEM((group, n_blocks), i32),
            pltpu.VMEM((2 * STEP * group, VB), f32),
            pltpu.SMEM((n_vox * SLOTS + 3 * STEP,), i32),
            pltpu.SMEM((n_vox * SLOTS + 3 * STEP,), i32),
            pltpu.SemaphoreType.DMA((5,)),
            pltpu.SemaphoreType.DMA((2,)),
        ],
        compiler_params=all_vmem,
    )(pattern.T, delays.T, apod.T, echoes)
    slots, later_rank, later_start = lax.optimization_barrier((slots, clutter_rank, start_block))
    wide_start = jnp.broadcast_to(later_start.T[:, :, None], (start_block.shape[1], frames, VB))
    parts = lax.all_to_all(slots, "vox", split_axis=0, concat_axis=0, tiled=True)
    placed, kept = pl.pallas_call(
        place_kernel,
        out_shape=(
            jax.ShapeDtypeStruct((n_own, f_dev, VB), f32),
            jax.ShapeDtypeStruct((start_block.shape[1], VB), f32),
        ),
        in_specs=[smem, vmem, vmem],
        out_specs=(vmem, vmem),
        scratch_shapes=[pltpu.VMEM((n_own, SLOTS, n_vox, VB), f32)],
        compiler_params=params,
    )(later_rank, pattern.T, parts.reshape(n_vox, SLOTS, f_dev, VB))

    def flipped(value, flip):
        return lax.ppermute(value, "frame", [(f, f ^ flip) for f in range(n_frame)])

    across = flipped(placed, 2)
    received = [placed, flipped(placed, 1), across, flipped(across, 1)]
    own_image, grams = pl.pallas_call(
        gram_kernel,
        out_shape=(
            jax.ShapeDtypeStruct((frames, VB), f32),
            jax.ShapeDtypeStruct((n_vox, f_dev, VB), f32),
        ),
        in_specs=[vmem] * n_frame,
        out_specs=(vmem, vmem),
        scratch_shapes=[pltpu.VMEM((n_frame, n_own, f_dev, VB), f32)],
        compiler_params=params,
    )(*received)
    grams = lax.all_to_all(grams, "vox", split_axis=0, concat_axis=0, tiled=True)
    return pl.pallas_call(
        subspace_kernel,
        out_shape=jax.ShapeDtypeStruct((frames, VB), f32),
        in_specs=[vmem, vmem, vmem, vmem],
        out_specs=vmem,
        scratch_shapes=[
            pltpu.VMEM((frames, frames), f32),
            pltpu.VMEM((start_block.shape[1], frames, VB), f32),
        ],
        compiler_params=params,
    )(grams, own_image, wide_start, kept)


def solution(mesh):
    placed = (P("frame", "vox", None), P(None, "vox"), P(None, "vox"), P(), P(), P())
    return jax.shard_map(
        per_device, mesh=mesh, in_specs=placed, out_specs=P(None, ("frame", "vox")), check_vma=False
    )
```
